768 devices in a mesh: batch: 96 (over z_lo, y, core), tensor: 8 (over z_hi, x).
Axes of the slice: x: 4, y: 8, z: 12 (z_hi: 2, z_lo: 6; z = z_hi * 6 + z_lo), core: 2. Of those that a mesh axis runs over, the one named last changes fastest.
Arguments:
- audio_hidden: bfloat16 [12288, 4096], P('batch'), may hold values from -9 to 9
- head_in: bfloat16 [4096, 1536], P(None, 'tensor'), may hold values from -1 to 1
- head_out: bfloat16 [1536, 1536], P('tensor'), may hold values from -1 to 1
- text_embed: bfloat16 [12288, 1536], P('batch'), may hold values from -6 to 6
- log_scale: float32 [], replicated, may hold values from 4.8 to 5.3
- pair_index: int32 [12288], P('batch'), may hold values from 0 to 12287, each once
- valid_count: int32 [96], replicated, may hold values from 32 to 128, as said below
Outputs:
- row_loss: float32 [12288], P(('batch', 'tensor'))
- grad_audio: float32 [12288, 1536], P(('batch', 'tensor'))
The draws below stay inside these ranges and needn't reach their ends.
Inputs may be any that keep to these rules, and one draw needn't show every extreme that they name: `valid_count`: one batch block has all 128 rows valid in every draw.
All inputs are finite; a program needn't handle non-finite values.
Results may differ from the reference program's by a relative error of at most 0.0064.
Values may be sent and summed in bfloat16 or wider, within the bound.
No kernel may reach another device: no remote copies, remote signals or barrier semaphores. Data moves between devices by JAX's collectives and lax.ppermute only.
A program may use at most 32 MiB of HBM per device.

```python
import jax
import jax.numpy as jnp
from jax import lax

H = 4096
E = 1536
PAIR_DEV = 128
PAIRS = 12288
N_BATCH = 96


def shared_weights(key):
    first = jnp.clip(jax.random.normal(jax.random.fold_in(key, 11), (H, E), jnp.float32), -4.0, 4.0) * H ** (-0.5)
    second = jnp.clip(jax.random.normal(jax.random.fold_in(key, 12), (E, E), jnp.float32), -4.0, 4.0) * E ** (-0.5)
    return (first, second)


def shared_audio(key):
    noise = jnp.clip(jax.random.normal(jax.random.fold_in(key, 13), (PAIRS, H), jnp.float32), -4.0, 4.0)
    audio = noise
    order = jax.random.permutation(jax.random.fold_in(key, 15), PAIRS)
    sources = order[:8]
    copies = order[8:16]
    steps_size = 0.04 * 1.3 ** jnp.arange(8, dtype=jnp.float32)
    nudge = jnp.clip(jax.random.normal(jax.random.fold_in(key, 16), (8, H), jnp.float32), -4.0, 4.0)
    audio = audio.at[copies].set(audio[sources] + steps_size[:, None] * nudge)
    audio = jnp.clip(audio, -9.0, 9.0)
    quarter = PAIR_DEV // 4
    slots = jax.random.permutation(jax.random.fold_in(key, 17), N_BATCH * quarter)[:16]
    queries = slots // quarter * PAIR_DEV + slots % quarter
    return (audio, sources, queries)


def embed_rows(rows, first, second):
    pre_act = jnp.dot(rows, first, precision=lax.Precision.HIGHEST)
    raw = jnp.dot(jax.nn.gelu(pre_act, approximate=False), second, precision=lax.Precision.HIGHEST)
    return raw * lax.rsqrt(jnp.sum(raw * raw, axis=1, keepdims=True) + 1e-06)


def draw_audio_hidden(key, part):
    audio, sources, queries = shared_audio(key)
    return audio.astype(jnp.bfloat16)


def draw_head_in(key, part):
    first, second = shared_weights(key)
    return first.astype(jnp.bfloat16)


def draw_head_out(key, part):
    first, second = shared_weights(key)
    return second.astype(jnp.bfloat16)


def draw_text_embed(key, part):
    first, second = shared_weights(key)
    audio, sources, queries = shared_audio(key)
    key = jax.random.fold_in(key, 2)
    text = jnp.clip(jax.random.normal(key, (PAIRS, E), jnp.float32), -6.0, 6.0)
    units = embed_rows(audio[sources], first, second)
    spread = 0.05 * 1.4 ** jnp.arange(8, dtype=jnp.float32)
    jitter = jnp.clip(jax.random.normal(jax.random.fold_in(key, 3), (8, E), jnp.float32), -4.0, 4.0)
    aligned = units * E ** 0.5 + spread[:, None] * jitter
    text = text.at[queries[:8]].set(aligned)
    return jnp.clip(text, -6.0, 6.0).astype(jnp.bfloat16)


def draw_valid_count(key, part):
    key = jax.random.fold_in(key, 1)
    first, second = jax.random.split(key)
    counts = jax.random.randint(first, (N_BATCH,), PAIR_DEV // 4, PAIR_DEV + 1)
    chosen = jax.random.randint(second, (), 0, N_BATCH)
    return jnp.where(jnp.arange(N_BATCH) == chosen, PAIR_DEV, counts).astype(jnp.int32)


def setup_inputs(seed: int = 0) -> dict:
    key_list = jax.random.split(jax.random.key(seed), 8)
    return {
        "audio_hidden": draw_audio_hidden(jax.random.fold_in(key_list[7], 71), 0),
        "head_in": draw_head_in(jax.random.fold_in(key_list[7], 71), 0),
        "head_out": draw_head_out(jax.random.fold_in(key_list[7], 71), 0),
        "text_embed": draw_text_embed(jax.random.fold_in(key_list[7], 71), 0),
        "log_scale": jnp.clip(jax.random.uniform(key_list[4], (), jnp.float32, 4.8, 5.3), 4.8, 5.3),
        "pair_index": jax.random.permutation(key_list[5], PAIRS).astype(jnp.int32),
        "valid_count": draw_valid_count(jax.random.fold_in(key_list[7], 71), 0),
    }


def unit_rows(values):
    return values * jax.lax.rsqrt(lax.optimization_barrier(jnp.sum(values * values, axis=1, keepdims=True)) + 1e-06)

def reference(audio_hidden, head_in, head_out, text_embed, log_scale, pair_index, valid_count):
    pre_act = jnp.dot(audio_hidden, head_in, preferred_element_type=jnp.float32)
    hidden = jax.nn.gelu(pre_act, approximate=False).astype(jnp.bfloat16)
    raw = jnp.dot(hidden, head_out, preferred_element_type=jnp.float32)
    audio_unit = unit_rows(raw).astype(jnp.bfloat16)
    text_unit = unit_rows(text_embed.astype(jnp.float32)).astype(jnp.bfloat16)
    scale = jnp.exp(log_scale)
    logits = scale * jnp.dot(text_unit, audio_unit.T, preferred_element_type=jnp.float32)
    positions = jnp.arange(PAIRS, dtype=jnp.int32)
    valid = positions % PAIR_DEV < valid_count[positions // PAIR_DEV]
    top = lax.optimization_barrier(jnp.max(logits, axis=1))
    total = jnp.log(lax.optimization_barrier(jnp.sum(jnp.exp(logits - top[:, None]), axis=1))) + top
    picked = jnp.take_along_axis(logits, pair_index[:, None], axis=1)[:, 0]
    row_loss = jnp.where(valid, total - picked, 0.0)
    onehot = (positions[None, :] == pair_index[:, None]).astype(logits.dtype)
    weights = jnp.where(valid[:, None], jnp.exp(logits - total[:, None]) - onehot, 0.0).astype(jnp.bfloat16)
    grad_audio = scale * jnp.dot(weights.T, text_unit, preferred_element_type=jnp.float32)
    return (row_loss, grad_audio)
```

```python
import jax
import jax.numpy as jnp
from jax import lax
from jax.sharding import Mesh, PartitionSpec as P

BATCH = ("zl", "y", "c")
TENSOR = ("zh", "x")
BF16 = jnp.bfloat16
F32 = jnp.float32


def unit_rows(values):
    return values * lax.rsqrt(jnp.sum(values * values, axis=1, keepdims=True) + 1e-06)


def swapped(value, axis):
    return lax.ppermute(value, axis, [(0, 1), (1, 0)])


def spread(value, axis, count):
    chunks = jnp.broadcast_to(value[None], (count,) + value.shape)
    return lax.all_to_all(chunks, axis, 0, 0)


def log_sum_exp(values, axis):
    top = jnp.max(values, axis=axis)
    return top + jnp.log(jnp.sum(jnp.exp(values - jnp.expand_dims(top, axis)), axis=axis))


def on_device(audio_hidden, head_in, head_out, text_embed, log_scale, pair_index, valid_count):
    rows, width = text_embed.shape
    n_zl, n_y, n_zh, n_x = (lax.axis_size(a) for a in ("zl", "y", "zh", "x"))
    zl, y, c, zh, x = (lax.axis_index(a) for a in ("zl", "y", "c", "zh", "x"))
    share = rows // (n_zh * n_x)
    scale = jnp.exp(log_scale)

    text_unit = unit_rows(text_embed.astype(F32)).astype(BF16)
    low = jnp.broadcast_to((pair_index % rows).astype(BF16)[None], (rows // 2, rows))
    high = jnp.broadcast_to((pair_index // rows).astype(BF16)[None], (rows // 2, rows))
    packed = jnp.concatenate([text_unit, jnp.concatenate([low, high], 0)], axis=1)
    text_all = lax.all_gather(packed, "y", axis=0, tiled=True)

    pre_act = jnp.dot(audio_hidden, head_in, preferred_element_type=F32)
    hidden = jax.nn.gelu(pre_act, approximate=False).astype(BF16)
    partial = jnp.dot(hidden, head_out, preferred_element_type=F32).astype(BF16)
    partial = partial.reshape(n_zh, n_x, share, width).transpose(1, 0, 2, 3)
    partial = lax.all_to_all(partial, "x", 0, 0)
    halves = jnp.sum(partial.astype(F32), axis=0)
    mine = jnp.where(zh == 0, halves[0], halves[1])
    other = jnp.where(zh == 0, halves[1], halves[0])
    raw = mine + swapped(other.astype(BF16), "zh").astype(F32)
    audio_unit = unit_rows(raw).astype(BF16)

    own = spread(audio_unit, "zl", n_zl).reshape(n_zl * share, width)
    audio = jnp.concatenate([own, swapped(own, "c")], axis=0)
    half = n_zl * share

    text = text_all[:, :width]
    extra = text_all[:, width:].reshape(n_y, rows, rows)
    low = extra[:, 0].astype(jnp.int32)
    high = extra[:, rows // 2].astype(jnp.int32)
    pair_c = high % 2
    pair_y = (high // 2) % n_y
    pair_zl = high // (2 * n_y)
    held = (pair_y == y) & (low // share == zh * n_x + x)
    column = jnp.where(pair_c == c, 0, half) + pair_zl * share + low % share
    column = jnp.where(held, column, -1).reshape(1, n_y * rows)
    onehot = lax.broadcasted_iota(jnp.int32, (2 * half, n_y * rows), 0) == column

    logits = scale * jnp.einsum("ae,te->at", audio, text, preferred_element_type=F32)
    local = log_sum_exp(logits, 0).reshape(n_y, rows)
    picked = jnp.sum(jnp.where(onehot, logits, 0.0), axis=0).reshape(n_y, rows)

    stats = spread(jnp.concatenate([local, picked], 0), ("y", "x"), n_y * n_x)
    local = log_sum_exp(stats[:, :n_y], 0)
    picked = jnp.sum(stats[:, n_y:], axis=0)
    both = swapped(jnp.concatenate([local, picked], 0), "zh")
    total = log_sum_exp(jnp.stack([local, both[:n_y]]), 0)
    picked = picked + both[n_y:]

    counts = lax.dynamic_slice_in_dim(valid_count.reshape(n_zl, n_y, 2), zl, 1, 0)[0]
    counts = jnp.where(c == 0, counts[:, 0], counts[:, 1])
    valid = lax.broadcasted_iota(jnp.int32, (n_y, rows), 1) < counts[:, None]
    losses = jnp.where(valid, total - picked, 0.0)
    losses = lax.dynamic_index_in_dim(losses, y, 0, False)
    row_loss = lax.dynamic_slice_in_dim(losses, (zh * n_x + x) * share, share, 0)

    weights = jnp.exp(logits - total.reshape(1, -1)) - onehot.astype(F32)
    weights = jnp.where(valid.reshape(1, -1), weights, 0.0).astype(BF16)
    terms = jnp.einsum("at,te->ae", weights, text, preferred_element_type=F32)
    kept = terms[:half] + swapped(terms[half:].astype(BF16), "c").astype(F32)
    parts = lax.all_to_all(kept.astype(BF16).reshape(n_zl, share, width), "zl", 0, 0)
    grad_audio = scale * jnp.sum(parts.astype(F32), axis=0)
    return (row_loss, grad_audio)


def build(mesh):
    placed = (
        P(BATCH, None),
        P(None, TENSOR),
        P(TENSOR, None),
        P(BATCH, None),
        P(),
        P(BATCH),
        P(),
    )
    return jax.shard_map(
        on_device,
        mesh=mesh,
        in_specs=placed,
        out_specs=(P(BATCH + TENSOR), P(BATCH + TENSOR, None)),
        check_vma=False,
    )


def solution(mesh):
    return build(Mesh(mesh.devices.reshape(6, 8, 2, 2, 4), BATCH + TENSOR))
```

```python
import jax
import jax.numpy as jnp
from jax import lax
from jax.sharding import Mesh, PartitionSpec as P

BATCH = ("zl", "y", "c")
TENSOR = ("zh", "x")
BF16 = jnp.bfloat16
F32 = jnp.float32


def unit_rows(values):
    return values * lax.rsqrt(jnp.sum(values * values, axis=1, keepdims=True) + 1e-06)


def swapped(value, axis):
    return lax.ppermute(value, axis, [(0, 1), (1, 0)])


def spread(value, axis, count):
    chunks = jnp.broadcast_to(value[None], (count,) + value.shape)
    return lax.all_to_all(chunks, axis, 0, 0)


def log_sum_exp(values, axis):
    top = jnp.max(values, axis=axis)
    return top + jnp.log(jnp.sum(jnp.exp(values - jnp.expand_dims(top, axis)), axis=axis))


def on_device(audio_hidden, head_in, head_out, text_embed, log_scale, pair_index, valid_count):
    rows, width = text_embed.shape
    n_zl, n_y, n_zh, n_x = (lax.axis_size(a) for a in ("zl", "y", "zh", "x"))
    zl, y, c, zh, x = (lax.axis_index(a) for a in ("zl", "y", "c", "zh", "x"))
    share = rows // (n_zh * n_x)
    scale = jnp.exp(log_scale)

    text_unit = unit_rows(text_embed.astype(F32)).astype(BF16)
    text = lax.all_gather(text_unit, "y", axis=0, tiled=True)
    pairs = spread(pair_index[None], "y", n_y).reshape(1, n_y * rows)

    pre_act = jnp.dot(audio_hidden, head_in, preferred_element_type=F32)
    hidden = jax.nn.gelu(pre_act, approximate=False).astype(BF16)
    partial = jnp.dot(hidden, head_out, preferred_element_type=F32).astype(BF16)
    partial = partial.reshape(n_zh, n_x, share, width).transpose(1, 0, 2, 3)
    partial = lax.all_to_all(partial, "x", 0, 0)
    halves = jnp.sum(partial.astype(F32), axis=0)
    mine = jnp.where(zh == 0, halves[0], halves[1])
    other = jnp.where(zh == 0, halves[1], halves[0])
    raw = mine + swapped(other.astype(BF16), "zh").astype(F32)
    audio_unit = unit_rows(raw).astype(BF16)

    own = spread(audio_unit, "zl", n_zl).reshape(n_zl * share, width)
    audio = jnp.concatenate([own, swapped(own, "c")], axis=0)
    half = n_zl * share

    low = pairs % rows
    high = pairs // rows
    pair_c = high % 2
    pair_y = (high // 2) % n_y
    pair_zl = high // (2 * n_y)
    held = (pair_y == y) & (low // share == zh * n_x + x)
    column = jnp.where(pair_c == c, 0, half) + pair_zl * share + low % share
    column = jnp.where(held, column, -1)
    onehot = lax.broadcasted_iota(jnp.int32, (2 * half, n_y * rows), 0) == column

    logits = scale * jnp.einsum("ae,te->at", audio, text, preferred_element_type=F32)
    local = log_sum_exp(logits, 0).reshape(n_y, rows)
    group = ("y", "zh", "x")
    total = log_sum_exp(spread(local, group, n_y * n_zh * n_x), 0)
    picked = jnp.sum(jnp.where(onehot, logits, 0.0), axis=0).reshape(-1, 1, share)
    picked = jnp.sum(lax.all_to_all(picked, group, 0, 0), axis=0)[0]

    counts = lax.dynamic_slice_in_dim(valid_count.reshape(n_zl, n_y, 2), zl, 1, 0)[0]
    counts = jnp.where(c == 0, counts[:, 0], counts[:, 1])
    valid = lax.broadcasted_iota(jnp.int32, (n_y, rows), 1) < counts[:, None]
    first = (zh * n_x + x) * share
    own_total = lax.dynamic_index_in_dim(total, y, 0, False)
    own_total = lax.dynamic_slice_in_dim(own_total, first, share, 0)
    own_count = lax.dynamic_index_in_dim(counts, y, 0, False)
    own_valid = first + jnp.arange(share, dtype=jnp.int32) < own_count
    row_loss = jnp.where(own_valid, own_total - picked, 0.0)

    weights = jnp.exp(logits - total.reshape(1, -1)) - onehot.astype(F32)
    weights = jnp.where(valid.reshape(1, -1), weights, 0.0).astype(BF16)
    sent = jnp.einsum("at,te->ae", weights[half:], text, preferred_element_type=F32)
    sent = swapped(sent.astype(BF16), "c")
    kept = jnp.einsum("at,te->ae", weights[:half], text, preferred_element_type=F32)
    kept = kept + sent.astype(F32)
    parts = lax.all_to_all(kept.astype(BF16).reshape(n_zl, share, width), "zl", 0, 0)
    grad_audio = scale * jnp.sum(parts.astype(F32), axis=0)
    return (row_loss, grad_audio)


def build(mesh):
    placed = (
        P(BATCH, None),
        P(None, TENSOR),
        P(TENSOR, None),
        P(BATCH, None),
        P(),
        P(BATCH),
        P(),
    )
    return jax.shard_map(
        on_device,
        mesh=mesh,
        in_specs=placed,
        out_specs=(P(BATCH + TENSOR), P(BATCH + TENSOR, None)),
        check_vma=False,
    )


def solution(mesh):
    return build(Mesh(mesh.devices.reshape(6, 8, 2, 2, 4), BATCH + TENSOR))
```

```python
import jax
import jax.numpy as jnp
from jax import lax
from jax.sharding import Mesh, PartitionSpec as P

BATCH = ("zl", "y", "c")
TENSOR = ("zh", "x")
BF16 = jnp.bfloat16
F32 = jnp.float32


def unit_rows(values):
    return values * lax.rsqrt(jnp.sum(values * values, axis=1, keepdims=True) + 1e-06)


def swapped(value, axis):
    return lax.ppermute(value, axis, [(0, 1), (1, 0)])


def spread(value, axis, count):
    chunks = jnp.broadcast_to(value[None], (count,) + value.shape)
    return lax.all_to_all(chunks, axis, 0, 0)


def log_sum_exp(values, axis):
    top = jnp.max(values, axis=axis)
    return top + jnp.log(jnp.sum(jnp.exp(values - jnp.expand_dims(top, axis)), axis=axis))


def on_device(audio_hidden, head_in, head_out, text_embed, log_scale, pair_index, valid_count):
    rows, width = text_embed.shape
    n_zl, n_y, n_zh, n_x = (lax.axis_size(a) for a in ("zl", "y", "zh", "x"))
    zl, y, c, zh, x = (lax.axis_index(a) for a in ("zl", "y", "c", "zh", "x"))
    share = rows // (n_zh * n_x)
    scale = jnp.exp(log_scale)

    text_unit = unit_rows(text_embed.astype(F32)).astype(BF16)
    low = jnp.broadcast_to((pair_index % rows).astype(BF16)[None], (rows // 2, rows))
    high = jnp.broadcast_to((pair_index // rows).astype(BF16)[None], (rows // 2, rows))
    packed = jnp.concatenate([text_unit, jnp.concatenate([low, high], 0)], axis=1)
    text_all = lax.all_gather(packed, "y", axis=0, tiled=True)

    pre_act = jnp.dot(audio_hidden, head_in, preferred_element_type=F32)
    hidden = jax.nn.gelu(pre_act, approximate=False).astype(BF16)
    partial = jnp.dot(hidden, head_out, preferred_element_type=F32).astype(BF16)
    partial = partial.reshape(n_zh, n_x, share, width).transpose(1, 0, 2, 3)
    partial = lax.all_to_all(partial, "x", 0, 0)
    halves = jnp.sum(partial.astype(F32), axis=0)
    mine = jnp.where(zh == 0, halves[0], halves[1])
    other = jnp.where(zh == 0, halves[1], halves[0])
    halves = jnp.concatenate([mine, other], axis=0)
    crossed = swapped(jnp.concatenate([other, mine], axis=0).astype(BF16), "zh")
    audio_unit = unit_rows(halves + crossed.astype(F32)).astype(BF16)

    own = spread(audio_unit, "zl", n_zl).reshape(2 * n_zl * share, width)
    audio = jnp.concatenate([own, swapped(own, "c")], axis=0)
    half = n_zl * share

    text = text_all[:, :width]
    extra = text_all[:, width:].reshape(n_y, rows, rows)
    low = extra[:, 0].astype(jnp.int32)
    high = extra[:, rows // 2].astype(jnp.int32)
    pair_c = high % 2
    pair_y = (high // 2) % n_y
    pair_zl = high // (2 * n_y)
    pair_t = low // share
    held = (pair_y == y) & (pair_t % n_x == x)
    near = pair_t // n_x == zh
    column = jnp.where(pair_c == c, 0, 2 * half) + pair_zl * 2 * share + low % share
    column = jnp.where(held, column + jnp.where(near, 0, share), -1).reshape(1, n_y * rows)
    onehot = lax.broadcasted_iota(jnp.int32, (4 * half, n_y * rows), 0) == column

    logits = scale * jnp.einsum("ae,te->at", audio, text, preferred_element_type=F32)
    local = log_sum_exp(logits, 0).reshape(1, 1, n_y * rows)
    picked = jnp.sum(jnp.where(onehot, logits, 0.0), axis=0).reshape(n_y, n_zh, n_x, share)
    picked = jnp.where(zh == 0, picked[:, 0], picked[:, 1]).reshape(n_y * n_x, 1, share)
    picked = jnp.pad(picked, ((0, 0), (0, 0), (0, rows - share)))
    chunks = jnp.broadcast_to(local, (n_y * n_x, 1, n_y * rows))
    stats = lax.all_to_all(jnp.concatenate([chunks, picked], 2), ("y", "x"), 0, 0)
    total = log_sum_exp(stats[:, 0, : n_y * rows], 0).reshape(n_y, rows)
    picked = jnp.sum(stats[:, 0, n_y * rows : n_y * rows + share], axis=0)

    counts = lax.dynamic_slice_in_dim(valid_count.reshape(n_zl, n_y, 2), zl, 1, 0)[0]
    counts = jnp.where(c == 0, counts[:, 0], counts[:, 1])
    valid = lax.broadcasted_iota(jnp.int32, (n_y, rows), 1) < counts[:, None]
    first = (zh * n_x + x) * share
    own_total = lax.dynamic_index_in_dim(total, y, 0, False)
    own_total = lax.dynamic_slice_in_dim(own_total, first, share, 0)
    own_count = lax.dynamic_index_in_dim(counts, y, 0, False)
    own_valid = first + jnp.arange(share, dtype=jnp.int32) < own_count
    row_loss = jnp.where(own_valid, own_total - picked, 0.0)

    def kept_rows(values):
        return values.reshape(2 * n_zl, 2, share, -1)[:, 0].reshape(2 * half, -1)

    weights = jnp.exp(kept_rows(logits) - total.reshape(1, -1)) - kept_rows(onehot).astype(F32)
    weights = jnp.where(valid.reshape(1, -1), weights, 0.0).astype(BF16)
    terms = jnp.einsum("at,te->ae", weights, text, preferred_element_type=F32)
    kept = terms[:half] + swapped(terms[half:].astype(BF16), "c").astype(F32)
    parts = lax.all_to_all(kept.astype(BF16).reshape(n_zl, share, width), "zl", 0, 0)
    grad_audio = scale * jnp.sum(parts.astype(F32), axis=0)
    return (row_loss, grad_audio)


def build(mesh):
    placed = (
        P(BATCH, None),
        P(None, TENSOR),
        P(TENSOR, None),
        P(BATCH, None),
        P(),
        P(BATCH),
        P(),
    )
    return jax.shard_map(
        on_device,
        mesh=mesh,
        in_specs=placed,
        out_specs=(P(BATCH + TENSOR), P(BATCH + TENSOR, None)),
        check_vma=False,
    )


def solution(mesh):
    return build(Mesh(mesh.devices.reshape(6, 8, 2, 2, 4), BATCH + TENSOR))
```

```python
import functools

import jax
import jax.numpy as jnp
from jax import lax
from jax.experimental import pallas as pl
from jax.experimental.pallas import tpu as pltpu
from jax.sharding import Mesh, PartitionSpec as P

BATCH = ("zl", "y", "c")
TENSOR = ("zh", "x")
BF16 = jnp.bfloat16
F32 = jnp.float32
I32 = jnp.int32
VMEM = pl.BlockSpec(memory_space=pltpu.VMEM)
HBM = pl.BlockSpec(memory_space=pl.ANY)
SMEM = pl.BlockSpec(memory_space=pltpu.SMEM)
LAST = (((1,), (1,)), ((), ()))
INNER = (((1,), (0,)), ((), ()))


def unit_rows(values):
    return values * lax.rsqrt(jnp.sum(values * values, axis=1, keepdims=True) + 1e-06)


def swapped(value, axis):
    return lax.ppermute(value, axis, [(0, 1), (1, 0)])


def spread(value, axis, count):
    chunks = jnp.broadcast_to(value[None], (count,) + value.shape)
    return lax.all_to_all(chunks, axis, 0, 0)


def started(sems, *pairs):
    copies = [pltpu.make_async_copy(a, b, sems.at[i]) for i, (a, b) in enumerate(pairs)]
    for copy in copies:
        copy.start()
    return copies


def pack_kernel(text_hbm, pair_hbm, out_ref, text_ref, pair_ref, sems):
    rows, width = text_ref.shape
    text_copy, pair_copy = started(sems, (text_hbm, text_ref), (pair_hbm, pair_ref))
    pair_copy.wait()
    pair = pair_ref[...]
    half = rows // 2
    low = lax.rem(pair, rows).astype(F32)
    high = lax.div(pair, rows).astype(F32)
    out_ref[:half, width:] = jnp.broadcast_to(low, (half, rows)).astype(BF16)
    out_ref[half:, width:] = jnp.broadcast_to(high, (half, rows)).astype(BF16)
    text_copy.wait()
    out_ref[:, :width] = unit_rows(text_ref[...].astype(F32)).astype(BF16)


def head_kernel(audio_hbm, first_hbm, second_hbm, out_ref, audio_ref, first_ref, second_ref, sems):
    n_x, n_zh, share, _ = out_ref.shape
    depth = audio_ref.shape[1]
    pieces = 4
    spans = [pl.ds(i * depth // pieces, depth // pieces) for i in range(pieces)]
    pairs = []
    for span in spans:
        pairs.append((audio_hbm.at[:, span], audio_ref.at[:, span]))
        pairs.append((first_hbm.at[:, span], first_ref.at[:, span]))
    copies = started(sems, *pairs, (second_hbm, second_ref))
    pre_act = 0.0
    for i, span in enumerate(spans):
        copies[2 * i].wait()
        copies[2 * i + 1].wait()
        pre_act += lax.dot_general(audio_ref[:, span], first_ref[:, span], LAST, preferred_element_type=F32)
    hidden = 0.5 * pre_act * (1.0 + lax.erf(pre_act * 0.7071067811865476))
    copies[-1].wait()
    partial = lax.dot_general(
        hidden.astype(BF16), second_ref[...], INNER, preferred_element_type=F32
    ).astype(BF16)
    for zh in range(n_zh):
        for x in range(n_x):
            start = (zh * n_x + x) * share
            out_ref[x, zh] = partial[start : start + share]


def pair_columns(text_ref, block, rows, width, place, sizes, share):
    zl, y, c, zh, x = place
    n_y, n_x = sizes
    start = block * rows
    low = text_ref[start : start + 16, width:].astype(F32)[0:1].astype(I32)
    start = start + rows // 2
    high = text_ref[start : start + 16, width:].astype(F32)[0:1].astype(I32)
    pair_t = lax.div(low, share)
    held = (lax.rem(lax.div(high, 2), n_y) == y) & (lax.rem(pair_t, n_x) == x)
    column = lax.div(high, 2 * n_y) * share + lax.rem(low, share)
    near_c = lax.rem(high, 2) == c
    return held, column, near_c, lax.div(pair_t, n_x)


def logits_kernel(place_ref, scale_ref, own_ref, other_ref, text_ref, kept_ref, stats_ref, *, sizes, share):
    n_y, n_x = sizes
    audio_rows, width = own_ref.shape
    rows = text_ref.shape[0] // n_y
    place = tuple(place_ref[i] for i in range(5))
    scale = scale_ref[0]
    n_zl = audio_rows // (2 * share)
    step = 2 * rows
    zh = place[3]
    row_ids = lax.broadcasted_iota(I32, (audio_rows, step), 0)
    for q in range(n_y // 2):
        span = slice(q * step, (q + 1) * step)
        text = text_ref[span, :width]
        parts = [pair_columns(text_ref, 2 * q + i, rows, width, place, sizes, share) for i in range(2)]
        wanted = []
        for near in (True, False):
            columns = []
            for held, column, near_c, pair_zh in parts:
                block = lax.div(column, share)
                spot = block * 2 * share + lax.rem(column, share) + pair_zh * share
                columns.append(jnp.where(held & (near_c == near), spot, -1))
            wanted.append(jnp.concatenate(columns, axis=1))
        logits = []
        picked = jnp.zeros((1, step), F32)
        for half, (ref, column) in enumerate(zip((own_ref, other_ref), wanted)):
            part = scale * lax.dot_general(ref[...], text, LAST, preferred_element_type=F32)
            logits.append(part)
            picked += jnp.sum(jnp.where(row_ids == column, part, 0.0), axis=0, keepdims=True)
            for zl in range(n_zl):
                to = (half * n_zl + zl) * share
                both = part[2 * zl * share : 2 * (zl + 1) * share]
                kept_ref[to : to + share, span] = jnp.where(zh == 0, both[:share], both[share:])
        top = functools.reduce(jnp.maximum, [jnp.max(p, axis=0, keepdims=True) for p in logits])
        mass = sum(jnp.sum(jnp.exp(p - top), axis=0, keepdims=True) for p in logits)
        local = top + jnp.log(mass)
        stats_ref[:, :, span] = jnp.broadcast_to(local[None], (n_y * n_x, 1, step))
        for i in range(2):
            first = (2 * q + i) * n_x
            block = picked[:, i * rows : (i + 1) * rows]
            stats_ref[first : first + n_x, :, n_y * rows :] = jnp.broadcast_to(block[None], (n_x, 1, rows))


def terms_kernel(place_ref, count_ref, stats_ref, kept_ref, text_ref, loss_ref, near_ref, far_ref, weight_ref, *, sizes, share):
    n_y, n_x = sizes
    audio_rows, width = kept_ref.shape[0], near_ref.shape[1]
    rows = text_ref.shape[0] // n_y
    half = audio_rows // 2
    place = tuple(place_ref[i] for i in range(5))
    zl, y, c, zh, x = place
    stats = stats_ref[:, :, : n_y * rows]
    top = jnp.max(stats, axis=0)
    total = top + jnp.log(jnp.sum(jnp.exp(stats - top[None]), axis=0))
    picked = jnp.sum(stats_ref[:, :, n_y * rows :], axis=0)
    row_ids = lax.broadcasted_iota(I32, (audio_rows, rows), 0)
    lane_ids = lax.broadcasted_iota(I32, (1, rows), 1)
    loss = jnp.zeros((1, rows), F32)
    for block in range(n_y):
        span = slice(block * rows, (block + 1) * rows)
        valid = lane_ids < count_ref[(zl * n_y + block) * 2 + c]
        loss = jnp.where(valid & (y == block), total[:, span] - picked, loss)
        held, column, near_c, pair_zh = pair_columns(text_ref, block, rows, width, place, sizes, share)
        column = jnp.where(held & (pair_zh == zh), column + jnp.where(near_c, 0, half), -1)
        weights = jnp.exp(kept_ref[:, span] - total[:, span]) - jnp.where(row_ids == column, 1.0, 0.0)
        weight_ref[:, span] = jnp.where(valid, weights, 0.0).astype(BF16)
    loss_ref[...] = loss
    step = 512 if width % 512 == 0 else width
    for start in range(0, width, step):
        span = slice(start, start + step)
        terms = lax.dot_general(weight_ref[...], text_ref[:, span], INNER, preferred_element_type=F32)
        near_ref[:, span] = terms[:half]
        far_ref[:, span] = terms[half:].astype(BF16)


def call(kernel, outs, specs, *args, vmem=32, scratch=(), flops=0, moved=0):
    return pl.pallas_call(
        kernel,
        out_shape=outs,
        in_specs=specs,
        out_specs=jax.tree.map(lambda _: VMEM, outs),
        scratch_shapes=scratch,
        compiler_params=pltpu.CompilerParams(vmem_limit_bytes=vmem * 2**20),
        cost_estimate=pl.CostEstimate(flops=flops, bytes_accessed=moved, transcendentals=0),
    )(*args)


def on_device(audio_hidden, head_in, head_out, text_embed, log_scale, pair_index, valid_count):
    rows, width = text_embed.shape
    n_zl, n_y, n_zh, n_x = (lax.axis_size(a) for a in ("zl", "y", "zh", "x"))
    place = [lax.axis_index(a) for a in BATCH + TENSOR]
    zl, y, c, zh, x = place
    place = jnp.stack(place).astype(I32)
    share = rows // (n_zh * n_x)
    sizes = (n_y, n_x)
    scale = jnp.exp(log_scale)
    out = jax.ShapeDtypeStruct

    packed = call(
        pack_kernel,
        out((rows, width + rows), BF16),
        [HBM, HBM],
        text_embed,
        pair_index.reshape(1, rows),
        vmem=62,
        scratch=[pltpu.VMEM((rows, width), BF16), pltpu.VMEM((1, rows), I32), pltpu.SemaphoreType.DMA((2,))],
        flops=4 * rows * width,
        moved=4 * rows * width,
    )
    text = lax.all_gather(packed, "y", axis=0, tiled=True)

    partial = call(
        head_kernel,
        out((n_x, n_zh, share, width), BF16),
        [HBM, HBM, HBM],
        audio_hidden,
        head_in.T,
        head_out,
        vmem=62,
        scratch=[
            pltpu.VMEM(audio_hidden.shape, BF16),
            pltpu.VMEM(head_in.shape[::-1], BF16),
            pltpu.VMEM(head_out.shape, BF16),
            pltpu.SemaphoreType.DMA((9,)),
        ],
        flops=2 * rows * head_in.shape[1] * (head_in.shape[0] + width),
        moved=2 * (audio_hidden.size + head_in.size + head_out.size),
    )
    partial = lax.all_to_all(partial, "x", 0, 0)
    halves = jnp.sum(partial.astype(F32), axis=0)
    mine = jnp.where(zh == 0, halves[0], halves[1])
    other = jnp.where(zh == 0, halves[1], halves[0])
    raw = mine + swapped(other.astype(BF16), "zh").astype(F32)
    audio_unit = unit_rows(raw).astype(BF16)

    own = spread(audio_unit, ("zl", "zh"), n_zl * n_zh).reshape(n_zl * n_zh * share, width)
    other = swapped(own, "c")
    half = n_zl * share

    kept, stats = call(
        functools.partial(logits_kernel, sizes=sizes, share=share),
        (out((2 * half, n_y * rows), F32), out((n_y * n_x, 1, (n_y + 1) * rows), F32)),
        [SMEM, SMEM, VMEM, VMEM, VMEM],
        place,
        scale.reshape(1),
        own,
        other,
        text,
        flops=8 * half * n_y * rows * width,
        moved=2 * text.size,
    )
    stats = lax.all_to_all(stats, ("y", "x"), 0, 0)
    losses, near, far = call(
        functools.partial(terms_kernel, sizes=sizes, share=share),
        (out((1, rows), F32), out((half, width), F32), out((half, width), BF16)),
        [SMEM, SMEM, VMEM, VMEM, VMEM],
        place,
        valid_count,
        stats,
        kept,
        text,
        scratch=[pltpu.VMEM((2 * half, n_y * rows), BF16)],
        flops=4 * half * n_y * rows * width,
        moved=2 * text.size,
    )
    row_loss = lax.dynamic_slice_in_dim(losses[0], (zh * n_x + x) * share, share, 0)
    near = near + swapped(far, "c").astype(F32)
    parts = lax.all_to_all(near.astype(BF16).reshape(n_zl, share, width), "zl", 0, 0)
    grad_audio = scale * jnp.sum(parts.astype(F32), axis=0)
    return (row_loss, grad_audio)


def build(mesh):
    placed = (
        P(BATCH, None),
        P(None, TENSOR),
        P(TENSOR, None),
        P(BATCH, None),
        P(),
        P(BATCH),
        P(),
    )
    return jax.shard_map(
        on_device,
        mesh=mesh,
        in_specs=placed,
        out_specs=(P(BATCH + TENSOR), P(BATCH + TENSOR, None)),
        check_vma=False,
    )


def solution(mesh):
    return build(Mesh(mesh.devices.reshape(6, 8, 2, 2, 4), BATCH + TENSOR))
```

```python
import functools

import jax
import jax.numpy as jnp
from jax import lax
from jax.experimental import pallas as pl
from jax.experimental.pallas import tpu as pltpu
from jax.sharding import Mesh, PartitionSpec as P

BATCH = ("zl", "y", "c")
TENSOR = ("zh", "x")
BF16 = jnp.bfloat16
F32 = jnp.float32
I32 = jnp.int32
VMEM = pl.BlockSpec(memory_space=pltpu.VMEM)
HBM = pl.BlockSpec(memory_space=pl.ANY)
SMEM = pl.BlockSpec(memory_space=pltpu.SMEM)
LAST = (((1,), (1,)), ((), ()))
INNER = (((1,), (0,)), ((), ()))


def unit_rows(values):
    return values * lax.rsqrt(jnp.sum(values * values, axis=1, keepdims=True) + 1e-06)


def swapped(value, axis):
    return lax.ppermute(value, axis, [(0, 1), (1, 0)])


def spread(value, axis, count):
    chunks = jnp.broadcast_to(value[None], (count,) + value.shape)
    return lax.all_to_all(chunks, axis, 0, 0)


def started(sems, *pairs):
    copies = [pltpu.make_async_copy(a, b, sems.at[i]) for i, (a, b) in enumerate(pairs)]
    for copy in copies:
        copy.start()
    return copies


def first_kernel(
    text_hbm, pair_hbm, audio_hbm, first_hbm, second_hbm, packed_ref, out_ref,
    text_ref, pair_ref, audio_ref, first_ref, second_ref, sems,
):
    rows, width = text_ref.shape
    n_x, n_zh, share, _ = out_ref.shape
    depth = audio_ref.shape[1]
    pieces = 4
    spans = [pl.ds(i * depth // pieces, depth // pieces) for i in range(pieces)]
    pairs = [(text_hbm, text_ref), (pair_hbm, pair_ref)]
    for span in spans:
        pairs.append((audio_hbm.at[:, span], audio_ref.at[:, span]))
        pairs.append((first_hbm.at[:, span], first_ref.at[:, span]))
    text_copy, pair_copy, *copies = started(sems, *pairs, (second_hbm, second_ref))
    pair_copy.wait()
    pair = pair_ref[...]
    half = rows // 2
    low = lax.rem(pair, rows).astype(F32)
    high = lax.div(pair, rows).astype(F32)
    packed_ref[:half, width:] = jnp.broadcast_to(low, (half, rows)).astype(BF16)
    packed_ref[half:, width:] = jnp.broadcast_to(high, (half, rows)).astype(BF16)
    text_copy.wait()
    packed_ref[:, :width] = unit_rows(text_ref[...].astype(F32)).astype(BF16)
    pre_act = 0.0
    for i, span in enumerate(spans):
        copies[2 * i].wait()
        copies[2 * i + 1].wait()
        pre_act += lax.dot_general(audio_ref[:, span], first_ref[:, span], LAST, preferred_element_type=F32)
    hidden = 0.5 * pre_act * (1.0 + lax.erf(pre_act * 0.7071067811865476))
    copies[-1].wait()
    partial = lax.dot_general(
        hidden.astype(BF16), second_ref[...], INNER, preferred_element_type=F32
    ).astype(BF16)
    for zh in range(n_zh):
        for x in range(n_x):
            start = (zh * n_x + x) * share
            out_ref[x, zh] = partial[start : start + share]


def pair_columns(text_ref, block, rows, width, place, sizes, share):
    zl, y, c, zh, x = place
    n_y, n_x = sizes
    start = block * rows
    low = text_ref[start : start + 16, width:].astype(F32)[0:1].astype(I32)
    start = start + rows // 2
    high = text_ref[start : start + 16, width:].astype(F32)[0:1].astype(I32)
    pair_t = lax.div(low, share)
    held = (lax.rem(lax.div(high, 2), n_y) == y) & (lax.rem(pair_t, n_x) == x)
    column = lax.div(high, 2 * n_y) * share + lax.rem(low, share)
    near_c = lax.rem(high, 2) == c
    return held, column, near_c, lax.div(pair_t, n_x)


def logits_kernel(scale_ref, audio_ref, text_ref, *refs, near, sizes, share):
    before, (kept_ref, stats_ref) = refs[:-2], refs[-2:]
    n_y, n_x = sizes
    audio_rows, width = audio_ref.shape
    rows = text_ref.shape[0] // n_y
    place = tuple(lax.axis_index(a) for a in BATCH + TENSOR)
    scale = scale_ref[0]
    n_zl = audio_rows // (2 * share)
    step = 2 * rows
    zh = place[3]
    row_ids = lax.broadcasted_iota(I32, (audio_rows, step), 0)
    for q in range(n_y // 2):
        span = slice(q * step, (q + 1) * step)
        columns = []
        for i in range(2):
            held, column, near_c, pair_zh = pair_columns(text_ref, 2 * q + i, rows, width, place, sizes, share)
            spot = lax.div(column, share) * 2 * share + lax.rem(column, share) + pair_zh * share
            columns.append(jnp.where(held & (near_c == near), spot, -1))
        column = jnp.concatenate(columns, axis=1)
        part = scale * lax.dot_general(
            audio_ref[...], text_ref[span, :width], LAST, preferred_element_type=F32
        )
        picked = jnp.sum(jnp.where(row_ids == column, part, 0.0), axis=0, keepdims=True)
        for zl in range(n_zl):
            both = part[2 * zl * share : 2 * (zl + 1) * share]
            kept_ref[zl * share : (zl + 1) * share, span] = jnp.where(zh == 0, both[:share], both[share:])
        top = jnp.max(part, axis=0, keepdims=True)
        if not before:
            stats_ref[0:1, span] = top
            stats_ref[1:2, span] = jnp.sum(jnp.exp(part - top), axis=0, keepdims=True)
            stats_ref[2:3, span] = picked
            continue
        top_before, mass, picked_before = (before[0][i : i + 1, span] for i in range(3))
        top = jnp.maximum(top, top_before)
        mass = mass * jnp.exp(top_before - top) + jnp.sum(jnp.exp(part - top), axis=0, keepdims=True)
        picked += picked_before
        local = top + jnp.log(mass)
        stats_ref[:, :, span] = jnp.broadcast_to(local[None], (n_y * n_x, 1, step))
        for i in range(2):
            first = (2 * q + i) * n_x
            block = picked[:, i * rows : (i + 1) * rows]
            stats_ref[first : first + n_x, :, n_y * rows :] = jnp.broadcast_to(block[None], (n_x, 1, rows))


def terms_kernel(count_ref, stats_ref, own_ref, other_ref, text_ref, loss_ref, near_ref, far_ref, weight_ref, *, sizes, share):
    n_y, n_x = sizes
    half, width = near_ref.shape
    rows = text_ref.shape[0] // n_y
    place = tuple(lax.axis_index(a) for a in BATCH + TENSOR)
    zl, y, c, zh, x = place
    stats = stats_ref[:, :, : n_y * rows]
    top = jnp.max(stats, axis=0)
    total = top + jnp.log(jnp.sum(jnp.exp(stats - top[None]), axis=0))
    picked = jnp.sum(stats_ref[:, :, n_y * rows :], axis=0)
    row_ids = lax.broadcasted_iota(I32, (half, rows), 0)
    lane_ids = lax.broadcasted_iota(I32, (1, rows), 1)
    loss = jnp.zeros((1, rows), F32)
    for block in range(n_y):
        span = slice(block * rows, (block + 1) * rows)
        valid = lane_ids < count_ref[(zl * n_y + block) * 2 + c]
        loss = jnp.where(valid & (y == block), total[:, span] - picked, loss)
        held, column, near_c, pair_zh = pair_columns(text_ref, block, rows, width, place, sizes, share)
        column = jnp.where(held & (pair_zh == zh), column, -1)
        for i, (ref, near) in enumerate(((own_ref, True), (other_ref, False))):
            hit = row_ids == jnp.where(near_c == near, column, -1)
            weights = jnp.exp(ref[:, span] - total[:, span]) - jnp.where(hit, 1.0, 0.0)
            weight_ref[i * half : (i + 1) * half, span] = jnp.where(valid, weights, 0.0).astype(BF16)
    loss_ref[...] = loss
    step = 512 if width % 512 == 0 else width
    for start in range(0, width, step):
        span = slice(start, start + step)
        terms = lax.dot_general(weight_ref[...], text_ref[:, span], INNER, preferred_element_type=F32)
        near_ref[:, span] = terms[:half]
        far_ref[:, span] = terms[half:].astype(BF16)


def call(kernel, outs, specs, *args, vmem=32, scratch=(), flops=0, moved=0):
    return pl.pallas_call(
        kernel,
        out_shape=outs,
        in_specs=specs,
        out_specs=jax.tree.map(lambda _: VMEM, outs),
        scratch_shapes=scratch,
        compiler_params=pltpu.CompilerParams(vmem_limit_bytes=vmem * 2**20),
        cost_estimate=pl.CostEstimate(flops=flops, bytes_accessed=moved, transcendentals=0),
    )(*args)


def on_device(audio_hidden, head_in, head_out, text_embed, log_scale, pair_index, valid_count):
    rows, width = text_embed.shape
    n_zl, n_y, n_zh, n_x = (lax.axis_size(a) for a in ("zl", "y", "zh", "x"))
    zh, x = lax.axis_index("zh"), lax.axis_index("x")
    share = rows // (n_zh * n_x)
    sizes = (n_y, n_x)
    scale = jnp.exp(log_scale)
    out = jax.ShapeDtypeStruct

    packed, partial = call(
        first_kernel,
        (out((rows, width + rows), BF16), out((n_x, n_zh, share, width), BF16)),
        [HBM] * 5,
        text_embed,
        pair_index.reshape(1, rows),
        audio_hidden,
        head_in.T,
        head_out,
        vmem=62,
        scratch=[
            pltpu.VMEM((rows, width), BF16),
            pltpu.VMEM((1, rows), I32),
            pltpu.VMEM(audio_hidden.shape, BF16),
            pltpu.VMEM(head_in.shape[::-1], BF16),
            pltpu.VMEM(head_out.shape, BF16),
            pltpu.SemaphoreType.DMA((11,)),
        ],
        flops=2 * rows * head_in.shape[1] * (head_in.shape[0] + width),
        moved=2 * (audio_hidden.size + head_in.size + head_out.size),
    )
    text = lax.all_gather(packed, "y", axis=0, tiled=True)

    partial = lax.all_to_all(partial, "x", 0, 0)
    halves = jnp.sum(partial.astype(F32), axis=0)
    mine = jnp.where(zh == 0, halves[0], halves[1])
    other = jnp.where(zh == 0, halves[1], halves[0])
    raw = mine + swapped(other.astype(BF16), "zh").astype(F32)
    audio_unit = unit_rows(raw).astype(BF16)

    own = spread(audio_unit, ("zl", "zh"), n_zl * n_zh).reshape(n_zl * n_zh * share, width)
    other = swapped(own, "c")
    half = n_zl * share

    def logits(near, audio, outs, *before):
        return call(
            functools.partial(logits_kernel, near=near, sizes=sizes, share=share),
            (out((half, n_y * rows), F32), outs),
            [SMEM] + [VMEM] * (2 + len(before)),
            scale.reshape(1),
            audio,
            text,
            *before,
            flops=4 * half * n_y * rows * width,
            moved=2 * text.size,
        )

    kept_own, sums = logits(True, own, out((8, n_y * rows), F32))
    kept_other, stats = logits(False, other, out((n_y * n_x, 1, (n_y + 1) * rows), F32), sums)
    stats = lax.all_to_all(stats, ("y", "x"), 0, 0)
    losses, near, far = call(
        functools.partial(terms_kernel, sizes=sizes, share=share),
        (out((1, rows), F32), out((half, width), F32), out((half, width), BF16)),
        [SMEM, VMEM, VMEM, VMEM, VMEM],
        valid_count,
        stats,
        kept_own,
        kept_other,
        text,
        scratch=[pltpu.VMEM((2 * half, n_y * rows), BF16)],
        flops=4 * half * n_y * rows * width,
        moved=2 * text.size,
    )
    row_loss = lax.dynamic_slice_in_dim(losses[0], (zh * n_x + x) * share, share, 0)
    near = near + swapped(far, "c").astype(F32)
    parts = lax.all_to_all(near.astype(BF16).reshape(n_zl, share, width), "zl", 0, 0)
    grad_audio = scale * jnp.sum(parts.astype(F32), axis=0)
    return (row_loss, grad_audio)


def build(mesh):
    placed = (
        P(BATCH, None),
        P(None, TENSOR),
        P(TENSOR, None),
        P(BATCH, None),
        P(),
        P(BATCH),
        P(),
    )
    return jax.shard_map(
        on_device,
        mesh=mesh,
        in_specs=placed,
        out_specs=(P(BATCH + TENSOR), P(BATCH + TENSOR, None)),
        check_vma=False,
    )


def solution(mesh):
    return build(Mesh(mesh.devices.reshape(6, 8, 2, 2, 4), BATCH + TENSOR))
```

```python
import functools

import jax
import jax.numpy as jnp
from jax import lax
from jax.experimental import pallas as pl
from jax.experimental.pallas import tpu as pltpu
from jax.sharding import Mesh, PartitionSpec as P

BATCH = ("zl", "y", "c")
TENSOR = ("zh", "x")
BF16 = jnp.bfloat16
F32 = jnp.float32
I32 = jnp.int32
VMEM = pl.BlockSpec(memory_space=pltpu.VMEM)
HBM = pl.BlockSpec(memory_space=pl.ANY)
SMEM = pl.BlockSpec(memory_space=pltpu.SMEM)
LAST = (((1,), (1,)), ((), ()))
INNER = (((1,), (0,)), ((), ()))


def unit_rows(values):
    return values * lax.rsqrt(jnp.sum(values * values, axis=1, keepdims=True) + 1e-06)


def swapped(value, axis):
    return lax.ppermute(value, axis, [(0, 1), (1, 0)])


def spread(value, axis, count):
    chunks = jnp.broadcast_to(value[None], (count,) + value.shape)
    return lax.all_to_all(chunks, axis, 0, 0)


def started(sems, *pairs):
    copies = [pltpu.make_async_copy(a, b, sems.at[i]) for i, (a, b) in enumerate(pairs)]
    for copy in copies:
        copy.start()
    return copies


def first_kernel(
    text_hbm, pair_hbm, audio_hbm, first_hbm, second_hbm, packed_ref, out_ref,
    text_ref, pair_ref, audio_ref, first_ref, second_ref, sems,
):
    rows, width = text_ref.shape
    n_x, n_zh, share, _ = out_ref.shape
    depth = audio_ref.shape[1]
    pieces = 4
    spans = [pl.ds(i * depth // pieces, depth // pieces) for i in range(pieces)]
    pairs = [(text_hbm, text_ref), (pair_hbm, pair_ref)]
    for span in spans:
        pairs.append((audio_hbm.at[:, span], audio_ref.at[:, span]))
        pairs.append((first_hbm.at[:, span], first_ref.at[:, span]))
    text_copy, pair_copy, *copies = started(sems, *pairs, (second_hbm, second_ref))
    pair_copy.wait()
    pair = pair_ref[...]
    half = rows // 2
    low = lax.rem(pair, rows).astype(F32)
    high = lax.div(pair, rows).astype(F32)
    packed_ref[:half, width:] = jnp.broadcast_to(low, (half, rows)).astype(BF16)
    packed_ref[half:, width:] = jnp.broadcast_to(high, (half, rows)).astype(BF16)
    text_copy.wait()
    packed_ref[:, :width] = unit_rows(text_ref[...].astype(F32)).astype(BF16)
    pre_act = 0.0
    for i, span in enumerate(spans):
        copies[2 * i].wait()
        copies[2 * i + 1].wait()
        pre_act += lax.dot_general(audio_ref[:, span], first_ref[:, span], LAST, preferred_element_type=F32)
    hidden = 0.5 * pre_act * (1.0 + lax.erf(pre_act * 0.7071067811865476))
    copies[-1].wait()
    partial = lax.dot_general(
        hidden.astype(BF16), second_ref[...], INNER, preferred_element_type=F32
    ).astype(BF16)
    for zh in range(n_zh):
        for x in range(n_x):
            start = (zh * n_x + x) * share
            out_ref[x, zh] = partial[start : start + share]


def pair_columns(text_ref, block, rows, width, place, sizes, share):
    zl, y, c, zh, x = place
    n_y, n_x = sizes
    start = block * rows
    low = text_ref[start : start + 16, width:].astype(F32)[0:1].astype(I32)
    start = start + rows // 2
    high = text_ref[start : start + 16, width:].astype(F32)[0:1].astype(I32)
    pair_t = lax.div(low, share)
    held = (lax.rem(lax.div(high, 2), n_y) == y) & (lax.rem(pair_t, n_x) == x)
    column = lax.div(high, 2 * n_y) * share + lax.rem(low, share)
    near_c = lax.rem(high, 2) == c
    return held, column, near_c, lax.div(pair_t, n_x)


def logits_kernel(scale_ref, audio_ref, text_ref, *refs, near, sizes, share):
    before, (kept_ref, stats_ref) = refs[:-2], refs[-2:]
    n_y, n_x = sizes
    audio_rows, width = audio_ref.shape
    rows = text_ref.shape[0] // n_y
    place = tuple(lax.axis_index(a) for a in BATCH + TENSOR)
    scale = scale_ref[...]
    n_zl = audio_rows // (2 * share)
    step = 2 * rows
    zh = place[3]
    row_ids = lax.broadcasted_iota(I32, (audio_rows, step), 0)
    for q in range(n_y // 2):
        span = slice(q * step, (q + 1) * step)
        columns = []
        for i in range(2):
            held, column, near_c, pair_zh = pair_columns(text_ref, 2 * q + i, rows, width, place, sizes, share)
            spot = lax.div(column, share) * 2 * share + lax.rem(column, share) + pair_zh * share
            columns.append(jnp.where(held & (near_c == near), spot, -1))
        column = jnp.concatenate(columns, axis=1)
        part = scale * lax.dot_general(
            audio_ref[...], text_ref[span, :width], LAST, preferred_element_type=F32
        )
        picked = jnp.sum(jnp.where(row_ids == column, part, 0.0), axis=0, keepdims=True)
        for zl in range(n_zl):
            both = part[2 * zl * share : 2 * (zl + 1) * share]
            kept_ref[zl * share : (zl + 1) * share, span] = jnp.where(zh == 0, both[:share], both[share:])
        top = jnp.max(part, axis=0, keepdims=True)
        if not before:
            stats_ref[0:1, span] = top
            stats_ref[1:2, span] = jnp.sum(jnp.exp(part - top), axis=0, keepdims=True)
            stats_ref[2:3, span] = picked
            continue
        top_before, mass, picked_before = (before[0][i : i + 1, span] for i in range(3))
        top = jnp.maximum(top, top_before)
        mass = mass * jnp.exp(top_before - top) + jnp.sum(jnp.exp(part - top), axis=0, keepdims=True)
        picked += picked_before
        local = top + jnp.log(mass)
        stats_ref[:, :, span] = jnp.broadcast_to(local[None], (n_y * n_x, 1, step))
        for i in range(2):
            first = (2 * q + i) * n_x
            block = picked[:, i * rows : (i + 1) * rows]
            stats_ref[first : first + n_x, :, n_y * rows :] = jnp.broadcast_to(block[None], (n_x, 1, rows))


def terms_kernel(count_ref, scale_ref, stats_ref, own_ref, other_ref, text_ref, loss_ref, near_ref, far_ref, weight_ref, *, sizes, share):
    n_y, n_x = sizes
    half, width = near_ref.shape
    rows = text_ref.shape[0] // n_y
    place = tuple(lax.axis_index(a) for a in BATCH + TENSOR)
    zl, y, c, zh, x = place
    stats = stats_ref[:, :, : n_y * rows]
    top = jnp.max(stats, axis=0)
    total = top + jnp.log(jnp.sum(jnp.exp(stats - top[None]), axis=0))
    picked = jnp.sum(stats_ref[:, :, n_y * rows :], axis=0)
    row_ids = lax.broadcasted_iota(I32, (half, rows), 0)
    lane_ids = lax.broadcasted_iota(I32, (1, rows), 1)
    loss = jnp.zeros((1, rows), F32)
    for block in range(n_y):
        span = slice(block * rows, (block + 1) * rows)
        valid = lane_ids < count_ref[(zl * n_y + block) * 2 + c]
        loss = jnp.where(valid & (y == block), total[:, span] - picked, loss)
        held, column, near_c, pair_zh = pair_columns(text_ref, block, rows, width, place, sizes, share)
        column = jnp.where(held & (pair_zh == zh), column, -1)
        for i, (ref, near) in enumerate(((own_ref, True), (other_ref, False))):
            hit = row_ids == jnp.where(near_c == near, column, -1)
            weights = jnp.exp(ref[:, span] - total[:, span]) - jnp.where(hit, 1.0, 0.0)
            weight_ref[i * half : (i + 1) * half, span] = jnp.where(valid, weights, 0.0).astype(BF16)
    first = (zh * n_x + x) * share
    loss_ref[...] = pltpu.roll(loss, lax.rem(rows - first, rows), 1)[:, :share]
    step = 512 if width % 512 == 0 else width
    for start in range(0, width, step):
        span = slice(start, start + step)
        terms = scale_ref[...] * lax.dot_general(
            weight_ref[...], text_ref[:, span], INNER, preferred_element_type=F32
        )
        near_ref[:, span] = terms[:half]
        far_ref[:, span] = terms[half:].astype(BF16)


def call(kernel, outs, specs, *args, vmem=32, scratch=(), flops=0, moved=0):
    return pl.pallas_call(
        kernel,
        out_shape=outs,
        in_specs=specs,
        out_specs=jax.tree.map(lambda _: VMEM, outs),
        scratch_shapes=scratch,
        compiler_params=pltpu.CompilerParams(vmem_limit_bytes=vmem * 2**20),
        cost_estimate=pl.CostEstimate(flops=flops, bytes_accessed=moved, transcendentals=0),
    )(*args)


def on_device(audio_hidden, head_in, head_out, text_embed, log_scale, pair_index, valid_count):
    rows, width = text_embed.shape
    n_zl, n_y, n_zh, n_x = (lax.axis_size(a) for a in ("zl", "y", "zh", "x"))
    zh = lax.axis_index("zh")
    share = rows // (n_zh * n_x)
    sizes = (n_y, n_x)
    scale = jnp.exp(log_scale).reshape(1, 1)
    out = jax.ShapeDtypeStruct

    packed, partial = call(
        first_kernel,
        (out((rows, width + rows), BF16), out((n_x, n_zh, share, width), BF16)),
        [HBM] * 5,
        text_embed,
        pair_index.reshape(1, rows),
        audio_hidden,
        head_in.T,
        head_out,
        vmem=62,
        scratch=[
            pltpu.VMEM((rows, width), BF16),
            pltpu.VMEM((1, rows), I32),
            pltpu.VMEM(audio_hidden.shape, BF16),
            pltpu.VMEM(head_in.shape[::-1], BF16),
            pltpu.VMEM(head_out.shape, BF16),
            pltpu.SemaphoreType.DMA((11,)),
        ],
        flops=2 * rows * head_in.shape[1] * (head_in.shape[0] + width),
        moved=2 * (audio_hidden.size + head_in.size + head_out.size),
    )
    text = lax.all_gather(packed, "y", axis=0, tiled=True)

    partial, scale = lax.optimization_barrier((lax.all_to_all(partial, "x", 0, 0), scale))
    halves = jnp.sum(partial.astype(F32), axis=0)
    mine = jnp.where(zh == 0, halves[0], halves[1])
    other = jnp.where(zh == 0, halves[1], halves[0])
    raw = mine + swapped(other.astype(BF16), "zh").astype(F32)
    audio_unit = unit_rows(raw).astype(BF16)

    own = spread(audio_unit, ("zl", "zh"), n_zl * n_zh).reshape(n_zl * n_zh * share, width)
    other = swapped(own, "c")
    half = n_zl * share

    def logits(near, audio, outs, *before):
        return call(
            functools.partial(logits_kernel, near=near, sizes=sizes, share=share),
            (out((half, n_y * rows), F32), outs),
            [VMEM] * (3 + len(before)),
            scale,
            audio,
            text,
            *before,
            flops=4 * half * n_y * rows * width,
            moved=2 * text.size,
        )

    kept_own, sums = logits(True, own, out((8, n_y * rows), F32))
    kept_other, stats = logits(False, other, out((n_y * n_x, 1, (n_y + 1) * rows), F32), sums)
    stats = lax.all_to_all(stats, ("y", "x"), 0, 0)
    losses, near, far = call(
        functools.partial(terms_kernel, sizes=sizes, share=share),
        (out((1, share), F32), out((half, width), F32), out((half, width), BF16)),
        [SMEM] + [VMEM] * 5,
        valid_count,
        scale,
        stats,
        kept_own,
        kept_other,
        text,
        scratch=[pltpu.VMEM((2 * half, n_y * rows), BF16)],
        flops=4 * half * n_y * rows * width,
        moved=2 * text.size,
    )
    near = near + swapped(far, "c").astype(F32)
    parts = lax.all_to_all(near.astype(BF16).reshape(n_zl, share, width), "zl", 0, 0)
    grad_audio = jnp.sum(parts.astype(F32), axis=0)
    return (losses[0], grad_audio)


def build(mesh):
    placed = (
        P(BATCH, None),
        P(None, TENSOR),
        P(TENSOR, None),
        P(BATCH, None),
        P(),
        P(BATCH),
        P(),
    )
    return jax.shard_map(
        on_device,
        mesh=mesh,
        in_specs=placed,
        out_specs=(P(BATCH + TENSOR), P(BATCH + TENSOR, None)),
        check_vma=False,
    )


def solution(mesh):
    return build(Mesh(mesh.devices.reshape(6, 8, 2, 2, 4), BATCH + TENSOR))
```

```python
import functools

import jax
import jax.numpy as jnp
from jax import lax
from jax.experimental import pallas as pl
from jax.experimental.pallas import tpu as pltpu
from jax.sharding import Mesh, PartitionSpec as P

BATCH = ("zl", "y", "c")
TENSOR = ("zh", "x")
BF16 = jnp.bfloat16
F32 = jnp.float32
I32 = jnp.int32
VMEM = pl.BlockSpec(memory_space=pltpu.VMEM)
HBM = pl.BlockSpec(memory_space=pl.ANY)
SMEM = pl.BlockSpec(memory_space=pltpu.SMEM)
LAST = (((1,), (1,)), ((), ()))
INNER = (((1,), (0,)), ((), ()))


def unit_rows(values):
    return values * lax.rsqrt(jnp.sum(values * values, axis=1, keepdims=True) + 1e-06)


def swapped(value, axis):
    return lax.ppermute(value, axis, [(0, 1), (1, 0)])


def spread(value, axis, count):
    chunks = jnp.broadcast_to(value[None], (count,) + value.shape)
    return lax.all_to_all(chunks, axis, 0, 0)


def started(sems, *pairs):
    copies = [pltpu.make_async_copy(a, b, sems.at[i]) for i, (a, b) in enumerate(pairs)]
    for copy in copies:
        copy.start()
    return copies


def first_kernel(
    text_hbm, pair_hbm, audio_hbm, first_hbm, second_hbm, packed_ref, out_ref,
    text_ref, pair_ref, audio_ref, first_ref, second_ref, sems,
):
    rows, width = text_ref.shape
    n_x, n_zh, share, _ = out_ref.shape
    depth = audio_ref.shape[1]
    pieces = 4
    spans = [pl.ds(i * depth // pieces, depth // pieces) for i in range(pieces)]
    pairs = [(text_hbm, text_ref), (pair_hbm, pair_ref)]
    for span in spans:
        pairs.append((audio_hbm.at[:, span], audio_ref.at[:, span]))
        pairs.append((first_hbm.at[:, span], first_ref.at[:, span]))
    text_copy, pair_copy, *copies = started(sems, *pairs, (second_hbm, second_ref))
    pair_copy.wait()
    pair = pair_ref[...]
    half = rows // 2
    low = lax.rem(pair, rows).astype(F32)
    high = lax.div(pair, rows).astype(F32)
    packed_ref[:half, width:] = jnp.broadcast_to(low, (half, rows)).astype(BF16)
    packed_ref[half:, width:] = jnp.broadcast_to(high, (half, rows)).astype(BF16)
    text_copy.wait()
    packed_ref[:, :width] = unit_rows(text_ref[...].astype(F32)).astype(BF16)
    pre_act = 0.0
    for i, span in enumerate(spans):
        copies[2 * i].wait()
        copies[2 * i + 1].wait()
        pre_act += lax.dot_general(audio_ref[:, span], first_ref[:, span], LAST, preferred_element_type=F32)
    hidden = 0.5 * pre_act * (1.0 + lax.erf(pre_act * 0.7071067811865476))
    copies[-1].wait()
    partial = lax.dot_general(
        hidden.astype(BF16), second_ref[...], INNER, preferred_element_type=F32
    ).astype(BF16)
    for zh in range(n_zh):
        for x in range(n_x):
            start = (zh * n_x + x) * share
            out_ref[x, zh] = partial[start : start + share]


def pair_columns(text_ref, block, rows, width, place, sizes, share):
    zl, y, c, zh, x = place
    n_y, n_x = sizes
    start = block * rows
    low = text_ref[start : start + 16, width:].astype(F32)[0:1].astype(I32)
    start = start + rows // 2
    high = text_ref[start : start + 16, width:].astype(F32)[0:1].astype(I32)
    pair_t = lax.div(low, share)
    held = (lax.rem(lax.div(high, 2), n_y) == y) & (lax.rem(pair_t, n_x) == x)
    column = lax.div(high, 2 * n_y) * share + lax.rem(low, share)
    near_c = lax.rem(high, 2) == c
    return held, column, near_c, lax.div(pair_t, n_x)


def logits_kernel(scale_ref, audio_ref, text_ref, *refs, near, sizes, share):
    before, (kept_ref, stats_ref) = refs[:-2], refs[-2:]
    n_y, n_x = sizes
    audio_rows, width = audio_ref.shape
    rows = text_ref.shape[0] // n_y
    place = tuple(lax.axis_index(a) for a in BATCH + TENSOR)
    scale = scale_ref[...]
    n_zl = audio_rows // (2 * share)
    step = 2 * rows
    zh = place[3]
    row_ids = lax.broadcasted_iota(I32, (audio_rows, step), 0)
    for q in range(n_y // 2):
        span = slice(q * step, (q + 1) * step)
        columns = []
        for i in range(2):
            held, column, near_c, pair_zh = pair_columns(text_ref, 2 * q + i, rows, width, place, sizes, share)
            spot = lax.div(column, share) * 2 * share + lax.rem(column, share) + pair_zh * share
            columns.append(jnp.where(held & (near_c == near), spot, -1))
        column = jnp.concatenate(columns, axis=1)
        part = scale * lax.dot_general(
            audio_ref[...], text_ref[span, :width], LAST, preferred_element_type=F32
        )
        picked = jnp.sum(jnp.where(row_ids == column, part, 0.0), axis=0, keepdims=True)
        for zl in range(n_zl):
            both = part[2 * zl * share : 2 * (zl + 1) * share]
            kept_ref[zl * share : (zl + 1) * share, span] = jnp.where(zh == 0, both[:share], both[share:])
        top = jnp.max(part, axis=0, keepdims=True)
        if not before:
            stats_ref[0:1, span] = top
            stats_ref[1:2, span] = jnp.sum(jnp.exp(part - top), axis=0, keepdims=True)
            stats_ref[2:3, span] = picked
            continue
        top_before, mass, picked_before = (before[0][i : i + 1, span] for i in range(3))
        top = jnp.maximum(top, top_before)
        mass = mass * jnp.exp(top_before - top) + jnp.sum(jnp.exp(part - top), axis=0, keepdims=True)
        picked += picked_before
        local = top + jnp.log(mass)
        stats_ref[:, :, span] = jnp.broadcast_to(local[None], (n_y * n_x, 1, step))
        for i in range(2):
            first = (2 * q + i) * n_x
            block = picked[:, i * rows : (i + 1) * rows]
            stats_ref[first : first + n_x, :, n_y * rows :] = jnp.broadcast_to(block[None], (n_x, 1, rows))


def terms_kernel(count_ref, scale_ref, stats_ref, kept_ref, text_ref, *refs, near, sizes, share):
    if near:
        total_ref, loss_ref, terms_ref, weight_ref = refs
    else:
        total_ref, terms_ref, weight_ref = refs
    n_y, n_x = sizes
    half, width = terms_ref.shape
    rows = text_ref.shape[0] // n_y
    zl, y, c, zh, x = place = tuple(lax.axis_index(a) for a in BATCH + TENSOR)
    if not near:
        stats = stats_ref[:, :, : n_y * rows]
        top = jnp.max(stats, axis=0)
        total_ref[...] = top + jnp.log(jnp.sum(jnp.exp(stats - top[None]), axis=0))
    total = total_ref[...]
    row_ids = lax.broadcasted_iota(I32, (half, rows), 0)
    lane_ids = lax.broadcasted_iota(I32, (1, rows), 1)
    if near:
        picked = jnp.sum(stats_ref[:, :, n_y * rows :], axis=0)
        loss = jnp.zeros((1, rows), F32)
    for block in range(n_y):
        span = slice(block * rows, (block + 1) * rows)
        valid = lane_ids < count_ref[(zl * n_y + block) * 2 + c]
        if near:
            loss = jnp.where(valid & (y == block), total[:, span] - picked, loss)
        held, column, near_c, pair_zh = pair_columns(text_ref, block, rows, width, place, sizes, share)
        hit = row_ids == jnp.where(held & (pair_zh == zh) & (near_c == near), column, -1)
        weights = jnp.exp(kept_ref[:, span] - total[:, span]) - jnp.where(hit, 1.0, 0.0)
        weight_ref[:, span] = jnp.where(valid, weights, 0.0).astype(BF16)
    if near:
        first = (zh * n_x + x) * share
        loss_ref[...] = pltpu.roll(loss, lax.rem(rows - first, rows), 1)[:, :share]
    step = 512 if width % 512 == 0 else width
    for start in range(0, width, step):
        span = slice(start, start + step)
        terms = scale_ref[...] * lax.dot_general(
            weight_ref[...], text_ref[:, span], INNER, preferred_element_type=F32
        )
        terms_ref[:, span] = terms.astype(terms_ref.dtype)


def call(kernel, outs, specs, *args, vmem=32, scratch=(), flops=0, moved=0):
    return pl.pallas_call(
        kernel,
        out_shape=outs,
        in_specs=specs,
        out_specs=jax.tree.map(lambda _: VMEM, outs),
        scratch_shapes=scratch,
        compiler_params=pltpu.CompilerParams(vmem_limit_bytes=vmem * 2**20),
        cost_estimate=pl.CostEstimate(flops=flops, bytes_accessed=moved, transcendentals=0),
    )(*args)


def on_device(audio_hidden, head_in, head_out, text_embed, log_scale, pair_index, valid_count):
    rows, width = text_embed.shape
    n_zl, n_y, n_zh, n_x = (lax.axis_size(a) for a in ("zl", "y", "zh", "x"))
    zh = lax.axis_index("zh")
    share = rows // (n_zh * n_x)
    sizes = (n_y, n_x)
    scale = jnp.exp(log_scale).reshape(1, 1)
    out = jax.ShapeDtypeStruct

    packed, partial = call(
        first_kernel,
        (out((rows, width + rows), BF16), out((n_x, n_zh, share, width), BF16)),
        [HBM] * 5,
        text_embed,
        pair_index.reshape(1, rows),
        audio_hidden,
        head_in.T,
        head_out,
        vmem=62,
        scratch=[
            pltpu.VMEM((rows, width), BF16),
            pltpu.VMEM((1, rows), I32),
            pltpu.VMEM(audio_hidden.shape, BF16),
            pltpu.VMEM(head_in.shape[::-1], BF16),
            pltpu.VMEM(head_out.shape, BF16),
            pltpu.SemaphoreType.DMA((11,)),
        ],
        flops=2 * rows * head_in.shape[1] * (head_in.shape[0] + width),
        moved=2 * (audio_hidden.size + head_in.size + head_out.size),
    )
    text = lax.all_gather(packed, "y", axis=0, tiled=True)

    partial, scale = lax.optimization_barrier((lax.all_to_all(partial, "x", 0, 0), scale))
    halves = jnp.sum(partial.astype(F32), axis=0)
    mine = jnp.where(zh == 0, halves[0], halves[1])
    other = jnp.where(zh == 0, halves[1], halves[0])
    raw = mine + swapped(other.astype(BF16), "zh").astype(F32)
    audio_unit = unit_rows(raw).astype(BF16)

    own = spread(audio_unit, ("zl", "zh"), n_zl * n_zh).reshape(n_zl * n_zh * share, width)
    other = swapped(own, "c")
    half = n_zl * share

    def logits(near, audio, outs, *before):
        return call(
            functools.partial(logits_kernel, near=near, sizes=sizes, share=share),
            (out((half, n_y * rows), F32), outs),
            [VMEM] * (3 + len(before)),
            scale,
            audio,
            text,
            *before,
            flops=4 * half * n_y * rows * width,
            moved=2 * text.size,
        )

    kept_own, sums = logits(True, own, out((8, n_y * rows), F32))
    kept_other, stats = logits(False, other, out((n_y * n_x, 1, (n_y + 1) * rows), F32), sums)
    stats = lax.all_to_all(stats, ("y", "x"), 0, 0)
    def terms(near, kept, outs, *before):
        return call(
            functools.partial(terms_kernel, near=near, sizes=sizes, share=share),
            outs,
            [SMEM] + [VMEM] * (4 + len(before)),
            valid_count,
            scale,
            stats,
            kept,
            text,
            *before,
            scratch=[pltpu.VMEM((half, n_y * rows), BF16)],
            flops=2 * half * n_y * rows * width,
            moved=2 * text.size,
        )

    total, far = terms(False, kept_other, (out((1, n_y * rows), F32), out((half, width), BF16)))
    far = swapped(far, "c")
    losses, near = terms(True, kept_own, (out((1, share), F32), out((half, width), F32)), total)
    near = near + far.astype(F32)
    parts = lax.all_to_all(near.astype(BF16).reshape(n_zl, share, width), "zl", 0, 0)
    grad_audio = jnp.sum(parts.astype(F32), axis=0)
    return (losses[0], grad_audio)


def build(mesh):
    placed = (
        P(BATCH, None),
        P(None, TENSOR),
        P(TENSOR, None),
        P(BATCH, None),
        P(),
        P(BATCH),
        P(),
    )
    return jax.shard_map(
        on_device,
        mesh=mesh,
        in_specs=placed,
        out_specs=(P(BATCH + TENSOR), P(BATCH + TENSOR, None)),
        check_vma=False,
    )


def solution(mesh):
    return build(Mesh(mesh.devices.reshape(6, 8, 2, 2, 4), BATCH + TENSOR))
```

```python
import functools

import jax
import jax.numpy as jnp
from jax import lax
from jax.experimental import pallas as pl
from jax.experimental.pallas import tpu as pltpu
from jax.sharding import Mesh, PartitionSpec as P

BATCH = ("zl", "y", "c")
TENSOR = ("zh", "x")
BF16 = jnp.bfloat16
F32 = jnp.float32
I32 = jnp.int32
VMEM = pl.BlockSpec(memory_space=pltpu.VMEM)
HBM = pl.BlockSpec(memory_space=pl.ANY)
SMEM = pl.BlockSpec(memory_space=pltpu.SMEM)
LAST = (((1,), (1,)), ((), ()))
INNER = (((1,), (0,)), ((), ()))


def unit_rows(values):
    return values * lax.rsqrt(jnp.sum(values * values, axis=1, keepdims=True) + 1e-06)


def swapped(value, axis):
    return lax.ppermute(value, axis, [(0, 1), (1, 0)])


def spread(value, axis, count):
    chunks = jnp.broadcast_to(value[None], (count,) + value.shape)
    return lax.all_to_all(chunks, axis, 0, 0)


def started(sems, *pairs):
    copies = [pltpu.make_async_copy(a, b, sems.at[i]) for i, (a, b) in enumerate(pairs)]
    for copy in copies:
        copy.start()
    return copies


def first_kernel(
    text_hbm, pair_hbm, audio_hbm, first_hbm, second_hbm, packed_ref, out_ref,
    text_ref, pair_ref, audio_ref, first_ref, second_ref, sems,
):
    rows, width = text_ref.shape
    n_x, n_zh, share, _ = out_ref.shape
    depth = audio_ref.shape[1]
    pieces = 2
    spans = [pl.ds(i * depth // pieces, depth // pieces) for i in range(pieces)]
    pairs = [(text_hbm, text_ref), (pair_hbm, pair_ref)]
    for span in spans:
        pairs.append((audio_hbm.at[:, span], audio_ref.at[:, span]))
        pairs.append((first_hbm.at[:, span], first_ref.at[:, span]))
    text_copy, pair_copy, *copies = started(sems, *pairs, (second_hbm, second_ref))
    pair_copy.wait()
    pair = pair_ref[...]
    half = rows // 2
    low = lax.rem(pair, rows).astype(F32)
    high = lax.div(pair, rows).astype(F32)
    packed_ref[:half, width:] = jnp.broadcast_to(low, (half, rows)).astype(BF16)
    packed_ref[half:, width:] = jnp.broadcast_to(high, (half, rows)).astype(BF16)
    text_copy.wait()
    packed_ref[:, :width] = unit_rows(text_ref[...].astype(F32)).astype(BF16)
    pre_act = 0.0
    for i, span in enumerate(spans):
        copies[2 * i].wait()
        copies[2 * i + 1].wait()
        pre_act += lax.dot_general(audio_ref[:, span], first_ref[:, span], LAST, preferred_element_type=F32)
    hidden = 0.5 * pre_act * (1.0 + lax.erf(pre_act * 0.7071067811865476))
    copies[-1].wait()
    partial = lax.dot_general(
        hidden.astype(BF16), second_ref[...], INNER, preferred_element_type=F32
    ).astype(BF16)
    for zh in range(n_zh):
        for x in range(n_x):
            start = (zh * n_x + x) * share
            out_ref[x, zh] = partial[start : start + share]


def pair_columns(text_ref, block, rows, width, place, sizes, share):
    zl, y, c, zh, x = place
    n_y, n_x = sizes
    start = block * rows
    low = text_ref[start : start + 16, width:].astype(F32)[0:1].astype(I32)
    start = start + rows // 2
    high = text_ref[start : start + 16, width:].astype(F32)[0:1].astype(I32)
    pair_t = lax.div(low, share)
    held = (lax.rem(lax.div(high, 2), n_y) == y) & (lax.rem(pair_t, n_x) == x)
    column = lax.div(high, 2 * n_y) * share + lax.rem(low, share)
    near_c = lax.rem(high, 2) == c
    return held, column, near_c, lax.div(pair_t, n_x)


def logits_kernel(scale_ref, audio_ref, text_ref, *refs, near, sizes, share):
    before, (kept_ref, stats_ref) = refs[:-2], refs[-2:]
    n_y, n_x = sizes
    audio_rows, width = audio_ref.shape
    rows = text_ref.shape[0] // n_y
    place = tuple(lax.axis_index(a) for a in BATCH + TENSOR)
    scale = scale_ref[...]
    step = 2 * rows
    zh = place[3]
    row_ids = lax.broadcasted_iota(I32, (audio_rows, step), 0)
    for q in range(n_y // 2):
        span = slice(q * step, (q + 1) * step)
        columns = []
        for i in range(2):
            held, column, near_c, pair_zh = pair_columns(text_ref, 2 * q + i, rows, width, place, sizes, share)
            spot = column + pair_zh * kept_ref.shape[0]
            columns.append(jnp.where(held & (near_c == near), spot, -1))
        column = jnp.concatenate(columns, axis=1)
        part = scale * lax.dot_general(
            audio_ref[...], text_ref[span, :width], LAST, preferred_element_type=F32
        )
        picked = jnp.sum(jnp.where(row_ids == column, part, 0.0), axis=0, keepdims=True)
        half = kept_ref.shape[0]
        kept_ref[:, span] = jnp.where(zh == 0, part[:half], part[half:])
        top = jnp.max(part, axis=0, keepdims=True)
        if not before:
            stats_ref[0:1, span] = top
            stats_ref[1:2, span] = jnp.sum(jnp.exp(part - top), axis=0, keepdims=True)
            stats_ref[2:3, span] = picked
            continue
        top_before, mass, picked_before = (before[0][i : i + 1, span] for i in range(3))
        top = jnp.maximum(top, top_before)
        mass = mass * jnp.exp(top_before - top) + jnp.sum(jnp.exp(part - top), axis=0, keepdims=True)
        picked += picked_before
        local = top + jnp.log(mass)
        stats_ref[:, :, span] = jnp.broadcast_to(local[None], (n_y * n_x, 1, step))
        for i in range(2):
            first = (2 * q + i) * n_x
            block = picked[:, i * rows : (i + 1) * rows]
            stats_ref[first : first + n_x, :, n_y * rows :] = jnp.broadcast_to(block[None], (n_x, 1, rows))


def terms_kernel(count_ref, scale_ref, stats_ref, own_ref, other_ref, text_ref, loss_ref, near_ref, far_ref, weight_ref, *, sizes, share):
    n_y, n_x = sizes
    half, width = near_ref.shape
    rows = text_ref.shape[0] // n_y
    place = tuple(lax.axis_index(a) for a in BATCH + TENSOR)
    zl, y, c, zh, x = place
    stats = stats_ref[:, :, : n_y * rows]
    top = jnp.max(stats, axis=0)
    total = top + jnp.log(jnp.sum(jnp.exp(stats - top[None]), axis=0))
    picked = jnp.sum(stats_ref[:, :, n_y * rows :], axis=0)
    row_ids = lax.broadcasted_iota(I32, (half, rows), 0)
    lane_ids = lax.broadcasted_iota(I32, (1, rows), 1)
    loss = jnp.zeros((1, rows), F32)
    for block in range(n_y):
        span = slice(block * rows, (block + 1) * rows)
        valid = lane_ids < count_ref[(zl * n_y + block) * 2 + c]
        loss = jnp.where(valid & (y == block), total[:, span] - picked, loss)
        held, column, near_c, pair_zh = pair_columns(text_ref, block, rows, width, place, sizes, share)
        column = jnp.where(held & (pair_zh == zh), column, -1)
        for i, (ref, near) in enumerate(((own_ref, True), (other_ref, False))):
            hit = row_ids == jnp.where(near_c == near, column, -1)
            weights = jnp.exp(ref[:, span] - total[:, span]) - jnp.where(hit, 1.0, 0.0)
            weight_ref[i * half : (i + 1) * half, span] = jnp.where(valid, weights, 0.0).astype(BF16)
    first = (zh * n_x + x) * share
    loss_ref[...] = pltpu.roll(loss, lax.rem(rows - first, rows), 1)[:, :share]
    step = 512 if width % 512 == 0 else width
    for start in range(0, width, step):
        span = slice(start, start + step)
        terms = scale_ref[...] * lax.dot_general(
            weight_ref[...], text_ref[:, span], INNER, preferred_element_type=F32
        )
        near_ref[:, span] = terms[:half]
        far_ref[:, span] = terms[half:].astype(BF16)


def call(kernel, outs, specs, *args, vmem=32, scratch=(), flops=0, moved=0):
    return pl.pallas_call(
        kernel,
        out_shape=outs,
        in_specs=specs,
        out_specs=jax.tree.map(lambda _: VMEM, outs),
        scratch_shapes=scratch,
        compiler_params=pltpu.CompilerParams(vmem_limit_bytes=vmem * 2**20),
        cost_estimate=pl.CostEstimate(flops=flops, bytes_accessed=moved, transcendentals=0),
    )(*args)


def on_device(audio_hidden, head_in, head_out, text_embed, log_scale, pair_index, valid_count):
    rows, width = text_embed.shape
    n_zl, n_y, n_zh, n_x = (lax.axis_size(a) for a in ("zl", "y", "zh", "x"))
    zh = lax.axis_index("zh")
    share = rows // (n_zh * n_x)
    sizes = (n_y, n_x)
    scale = jnp.exp(log_scale).reshape(1, 1)
    out = jax.ShapeDtypeStruct

    packed, partial = call(
        first_kernel,
        (out((rows, width + rows), BF16), out((n_x, n_zh, share, width), BF16)),
        [HBM] * 5,
        text_embed,
        pair_index.reshape(1, rows),
        audio_hidden,
        head_in.T,
        head_out,
        vmem=62,
        scratch=[
            pltpu.VMEM((rows, width), BF16),
            pltpu.VMEM((1, rows), I32),
            pltpu.VMEM(audio_hidden.shape, BF16),
            pltpu.VMEM(head_in.shape[::-1], BF16),
            pltpu.VMEM(head_out.shape, BF16),
            pltpu.SemaphoreType.DMA((7,)),
        ],
        flops=2 * rows * head_in.shape[1] * (head_in.shape[0] + width),
        moved=2 * (audio_hidden.size + head_in.size + head_out.size),
    )
    text = lax.all_gather(packed, "y", axis=0, tiled=True)

    partial, scale = lax.optimization_barrier((lax.all_to_all(partial, "x", 0, 0), scale))
    halves = jnp.sum(partial.astype(F32), axis=0)
    mine = jnp.where(zh == 0, halves[0], halves[1])
    other = jnp.where(zh == 0, halves[1], halves[0])
    raw = mine + swapped(other.astype(BF16), "zh").astype(F32)
    audio_unit = unit_rows(raw).astype(BF16)

    own = spread(audio_unit, ("zh", "zl"), n_zl * n_zh).reshape(n_zl * n_zh * share, width)
    other = swapped(own, "c")
    half = n_zl * share

    def logits(near, audio, outs, *before):
        return call(
            functools.partial(logits_kernel, near=near, sizes=sizes, share=share),
            (out((half, n_y * rows), F32), outs),
            [VMEM] * (3 + len(before)),
            scale,
            audio,
            text,
            *before,
            flops=4 * half * n_y * rows * width,
            moved=2 * text.size,
        )

    kept_own, sums = logits(True, own, out((8, n_y * rows), F32))
    kept_other, stats = logits(False, other, out((n_y * n_x, 1, (n_y + 1) * rows), F32), sums)
    stats = lax.all_to_all(stats, ("y", "x"), 0, 0)
    losses, near, far = call(
        functools.partial(terms_kernel, sizes=sizes, share=share),
        (out((1, share), F32), out((half, width), F32), out((half, width), BF16)),
        [SMEM] + [VMEM] * 5,
        valid_count,
        scale,
        stats,
        kept_own,
        kept_other,
        text,
        scratch=[pltpu.VMEM((2 * half, n_y * rows), BF16)],
        flops=4 * half * n_y * rows * width,
        moved=2 * text.size,
    )
    near = near + swapped(far, "c").astype(F32)
    parts = lax.all_to_all(near.astype(BF16).reshape(n_zl, share, width), "zl", 0, 0)
    grad_audio = jnp.sum(parts.astype(F32), axis=0)
    return (losses[0], grad_audio)


def build(mesh):
    placed = (
        P(BATCH, None),
        P(None, TENSOR),
        P(TENSOR, None),
        P(BATCH, None),
        P(),
        P(BATCH),
        P(),
    )
    return jax.shard_map(
        on_device,
        mesh=mesh,
        in_specs=placed,
        out_specs=(P(BATCH + TENSOR), P(BATCH + TENSOR, None)),
        check_vma=False,
    )


def solution(mesh):
    return build(Mesh(mesh.devices.reshape(6, 8, 2, 2, 4), BATCH + TENSOR))
```
